512 devices in a mesh: row: 16 (over z_hi, y), col: 16 (over x, z_lo), pair: 2 (over core).
Axes of the slice: x: 4, y: 4, z: 16 (z_hi: 4, z_lo: 4; z = z_hi * 4 + z_lo), core: 2. Of those that a mesh axis runs over, the one named last changes fastest.
Arguments:
- amplitudes: bfloat16 [24576, 2048], P(('row', 'col'), 'pair'), may hold values from -6 to 6
- integrals: bfloat16 [24576, 24576], P('row', 'col'), as said below
- virt_irrep: int32 [768], replicated, may hold values from 0 to 7, as said below
- pair_list: int32 [24576, 2], replicated, may hold values from 0 to 767
Outputs:
- residual: bfloat16 [24576, 2048], P(('col', 'row'), 'pair')
The draws below stay inside these ranges and needn't reach their ends.
Inputs may be any that keep to these rules, and one draw needn't show every extreme that they name: integrals is symmetric: integrals[p, q] = integrals[q, p]. `virt_irrep`: labels of the 8 irreps; every label occurs, their counts are uneven.
All inputs are finite; a program needn't handle non-finite values.
Results may differ from the reference program's by a relative error of at most 0.018.
Values may be sent and summed in bfloat16 or wider, within the bound.
No kernel may reach another device: no remote copies, remote signals or barrier semaphores. Data moves between devices by JAX's collectives and lax.ppermute only.
A program may use at most 64 MiB of HBM per device.

```python
import jax
import jax.numpy as jnp
from jax import lax

NV = 768
IRREPS = 8
BLK = 1536
PAIRS = 24576
NPAIRS = 2048
N_ROW = 16


def draw_integrals(key, part):
    key = jax.random.fold_in(key, 11)
    first = jax.random.fold_in(key, 0)
    scale = (0.15 * PAIRS) ** (-0.5)
    raw = jax.random.normal(first, (PAIRS, PAIRS), jnp.float32)
    mirrored = (raw + raw.T) * 0.5 ** 0.5 * scale
    return mirrored.astype(jnp.bfloat16)


def draw_virt_irrep(key, part):
    key = jax.random.fold_in(key, 23)
    first, second, third = jax.random.split(key, 3)
    lower = jax.random.randint(first, (NV,), 0, IRREPS)
    upper = jax.random.randint(second, (NV,), 0, IRREPS)
    labels = jnp.minimum(lower, upper)
    ranks = jax.random.permutation(third, jnp.arange(NV, dtype=jnp.int32))
    return jnp.where(ranks < IRREPS, ranks, labels).astype(jnp.int32)


def with_ends(drawn, rng, low, top_value):
    longest = drawn.shape.index(max(drawn.shape))
    spots = []
    for shift in (0, 1):
        where = [jax.random.randint(jax.random.fold_in(rng, axis), (), 0, length) for axis, length in enumerate(drawn.shape)]
        where[longest] = (where[longest] + shift) % drawn.shape[longest]
        spots.append(tuple(where))
    return drawn.at[spots[0]].set(low).at[spots[1]].set(top_value)


def steps_of(rng, extent, cuts, smallest, largest):
    def one(dim, parts):
        draws = jax.random.uniform(jax.random.fold_in(jax.random.fold_in(rng, 6), dim), (parts,), jnp.float32, smallest / len(cuts), largest / len(cuts))
        return jnp.repeat(jnp.exp(draws), extent[dim] // parts).reshape((-1,) + (1,) * (len(extent) - dim - 1))

    level = one(*cuts[0])
    for cut in cuts[1:]:
        level = level * one(*cut)
    return level


def centred(key, dims, scale, bound, pieces=(), held_as=jnp.bfloat16):
    entries = scale * jax.random.normal(key, dims, jnp.float32)
    if pieces:
        entries = entries * steps_of(key, dims, pieces, -0.22, 0.18)
    return jnp.clip(entries, -bound, bound).astype(held_as)


def setup_inputs(seed: int = 0) -> dict:
    seeds = jax.random.split(jax.random.key(seed), 5)
    amplitudes = centred(seeds[0], (PAIRS, NPAIRS), 1.0, 6.0, ((0, 256), (1, 2)))
    integrals = draw_integrals(jax.random.fold_in(seeds[4], 71), 0)
    virt_irrep = draw_virt_irrep(jax.random.fold_in(seeds[4], 71), 0)
    pair_list = with_ends(jax.random.randint(seeds[3], (PAIRS, 2), 0, NV), jax.random.fold_in(seeds[3], 1), 0, NV - 1).astype(jnp.int32)
    return {"amplitudes": amplitudes, "integrals": integrals, "virt_irrep": virt_irrep, "pair_list": pair_list}


def reference(amplitudes, integrals, virt_irrep, pair_list):
    symmetry = jnp.bitwise_xor(virt_irrep[pair_list[:, 0]], virt_irrep[pair_list[:, 1]]).astype(jnp.int32)
    total_pairs = integrals.shape[0]
    width = amplitudes.shape[1]

    def one_block(index, total):
        start = (index * BLK).astype(jnp.int32)
        columns = lax.dynamic_slice_in_dim(integrals, start, BLK, 1)
        column_symmetry = lax.dynamic_slice_in_dim(symmetry, start, BLK, 0)
        coupled = jnp.where(symmetry[:, None] == column_symmetry[None, :], columns, jnp.zeros((), columns.dtype))
        amps_block = lax.dynamic_slice_in_dim(amplitudes, start, BLK, 0)
        partial_value = jnp.dot(coupled.astype(jnp.float32), amps_block.astype(jnp.float32), precision=lax.Precision.HIGHEST)
        rounded = lax.optimization_barrier(partial_value.astype(jnp.bfloat16)).astype(jnp.float32)
        return total + rounded

    start_total = jnp.zeros((total_pairs, width), jnp.float32)
    result = lax.fori_loop(jnp.int32(0), jnp.int32(N_ROW), one_block, start_total)
    return result.astype(jnp.bfloat16)
```

```python
import jax
import jax.numpy as jnp
from jax import lax
from jax.sharding import Mesh, PartitionSpec as P

CHUNKS = 2


def pair_symmetry(pairs, labels):
    orbital = lax.broadcasted_iota(jnp.int32, (1, labels.shape[0]), 1)
    first = jnp.sum(jnp.where(pairs[:, 0:1] == orbital, labels[None, :], 0), axis=1)
    second = jnp.sum(jnp.where(pairs[:, 1:2] == orbital, labels[None, :], 0), axis=1)
    return jnp.bitwise_xor(first, second)


def shift(block, axis, first, second):
    moves = [
        (i * 2 + core, (i + step) % 4 * 2 + core)
        for i in range(4)
        for core, step in ((0, first), (1, second))
    ]
    return lax.ppermute(block, (axis, "core"), moves)


def pick(blocks, index):
    return lax.dynamic_index_in_dim(blocks, index % 4, 0, keepdims=False)


def total(*terms):
    return sum(t.astype(jnp.float32) for t in terms)


def gather_x(own):
    return jnp.concatenate(
        [own, shift(own, "x", 1, 1), shift(own, "x", -1, -1), shift(own, "x", 2, -2)], axis=0
    )


def scatter_y(partial, y):
    part = lambda d: lax.dynamic_index_in_dim(partial, (y + d) % 4, 1, keepdims=False)
    up = shift(part(1), "y", 1, 1)
    down = shift(part(3), "y", -1, -1)
    far = shift(part(2), "y", 2, -2)
    return total(part(0), up, down, far).astype(partial.dtype)


def scatter_zh(partial, zh, core):
    relayed = shift(pick(partial, zh + 2), "zh", 1, -1)
    add = lambda block, mine: jnp.where(mine, total(block, relayed), total(block)).astype(partial.dtype)
    up = shift(add(pick(partial, zh + 1), core == 0), "zh", 1, 1)
    down = shift(add(pick(partial, zh + 3), core == 1), "zh", -1, -1)
    return total(pick(partial, zh), up, down).astype(partial.dtype)


def body(amplitudes, integrals, virt_irrep, pair_list):
    blk = integrals.shape[0]
    zh, y, x, zl, core = (lax.axis_index(a) for a in ("zh", "y", "x", "zl", "core"))
    cd_pairs = lax.dynamic_slice_in_dim(pair_list, (zh * 4 + y) * blk, blk, 0)
    ab_pairs = lax.dynamic_slice_in_dim(pair_list, (x * 4 + zl) * blk, blk, 0)
    matching = (
        pair_symmetry(cd_pairs, virt_irrep)[:, None] == pair_symmetry(ab_pairs, virt_irrep)[None, :]
    )
    coupled = jnp.where(matching, integrals, jnp.zeros((), integrals.dtype)).reshape(4, -1, blk)
    coupled = lax.optimization_barrier(
        jnp.concatenate([pick(coupled, x + d) for d in (0, 3, 1, 2)], axis=0)
    )
    near = lax.all_gather(amplitudes, "zl", axis=0, tiled=True)
    width = amplitudes.shape[1] // CHUNKS
    done = []
    for k in range(CHUNKS):
        block = gather_x(near[:, k * width : (k + 1) * width])
        product = lax.dot_general(
            coupled, block, (((0,), (0,)), ((), ())), preferred_element_type=jnp.float32
        ).astype(jnp.bfloat16)
        product = lax.optimization_barrier(product).reshape(4, 4, -1, width)
        done.append(scatter_zh(scatter_y(product, y), zh, core))
    return jnp.concatenate(done, axis=1)


def solution(mesh):
    fine = Mesh(mesh.devices.reshape(4, 4, 4, 4, 2), ("zh", "y", "x", "zl", "core"))
    row, col = ("zh", "y"), ("x", "zl")
    placed = (P(row + col, "core"), P(row, col), P(), P())
    return jax.shard_map(
        body, mesh=fine, in_specs=placed, out_specs=P(col + row, "core"), check_vma=False
    )
```

```python
import functools

import jax
import jax.numpy as jnp
from jax import lax
from jax.experimental import pallas as pl
from jax.experimental.pallas import tpu as pltpu
from jax.sharding import Mesh, PartitionSpec as P

WIDTHS = (512, 512)
GATHER_X = ("dir", "dir")
SCATTER_Y = "dir"
SCATTER_Z = ('rl', 'rl')
TIE = True
COST = 100
VMEM = 24
PREP_FIRST = True
MERGE_Z = False


def permute(block, axis, target):
    moves = [(i * 2 + core, target(i, core) % 4 * 2 + core) for i in range(4) for core in (0, 1)]
    return lax.ppermute(block, (axis, "core"), moves)


def shift(block, axis, first, second):
    return permute(block, axis, lambda i, core: i + (second if core else first))


def swap(block, axis, first, second):
    return permute(block, axis, lambda i, core: i ^ (second if core else first))


def total(*terms):
    return sum(t.astype(jnp.float32) for t in terms)


def places(kind, me, core):
    if kind in ("dir", "rl"):
        return [(me + d) % 4 for d in range(4)]
    if kind == "rh":
        near = jnp.where(core == 0, 3, 1)
        return [me, me ^ near, me ^ near ^ 2, me ^ 2]
    return list(range(4))


def gather(kind, own, axis):
    if kind == "dir":
        far = shift(own, axis, 2, -2)
        after = shift(own, axis, -1, -1)
        return [own, after, far, shift(own, axis, 1, 1)]
    if kind == "rl":
        before, after = shift(own, axis, 1, 1), shift(own, axis, -1, -1)
        onward = jnp.where(lax.axis_index("core") == 0, before, after)
        return [own, after, shift(onward, axis, 1, -1), before]
    if kind == "rh":
        first = swap(own, axis, 1, 3)
        pair = swap(jnp.stack([own, first]), axis, 3, 1)
        return [own, pair[0], first, pair[1]]
    whole = lax.all_to_all(jnp.broadcast_to(own[None], (4,) + own.shape), axis, 0, 0)
    return [whole[i] for i in range(4)]


def scatter(kind, blocks, axis):
    dtype = blocks.dtype
    if kind == "dir":
        far = shift(blocks[2], axis, 2, -2)
        up = shift(blocks[1], axis, 1, 1)
        down = shift(blocks[3], axis, -1, -1)
        return total(blocks[0], far, up, down).astype(dtype)
    there = swap(blocks[2:], axis, 1, 3)
    kept = total(blocks[0], there[0])
    onward = total(blocks[1], there[1]).astype(dtype)
    return (kept + swap(onward, axis, 3, 1).astype(jnp.float32)).astype(dtype)


def pieces(blocks, order):
    return jnp.stack([lax.dynamic_index_in_dim(blocks, i, 0, keepdims=False) for i in order])


def lookup(table, index):
    found = jnp.zeros(index.shape, table.dtype)
    for row in range(table.shape[0]):
        line = jnp.broadcast_to(table[row : row + 1, :], index.shape)
        value = jnp.take_along_axis(line, index & 127, axis=1)
        found = jnp.where(index >> 7 == row, value, found)
    return found


def couple_kernel(rows_to, block, table, orbitals, out, labels):
    step = pl.program_id(0)
    tile, blk = block.shape[1], block.shape[0]
    lines = blk // 128

    @pl.when(step == 0)
    def _():
        symmetry = lookup(table[...], orbitals[...]).astype(jnp.float32)
        first, second = symmetry[: 2 * lines].astype(jnp.int32), symmetry[2 * lines :].astype(jnp.int32)
        labels[...] = jnp.bitwise_xor(first, second).astype(jnp.float32)

    mine = []
    for k in range(tile // 128):
        line = labels[pl.ds(step * (tile // 128) + k, 1), :]
        mine.append(jnp.broadcast_to(line, (128, 128)).T.astype(block.dtype))
    mine = jnp.concatenate(mine, axis=0)
    turned = block[...].T
    size = tile // 4
    for j in range(lines):
        across = slice(j * 128, (j + 1) * 128)
        other = labels[lines + j : lines + j + 1, :].astype(block.dtype)
        masked = jnp.where(mine == other, turned[:, across], jnp.zeros((), block.dtype))
        for k in range(4):
            out[rows_to[k], 0, :, across] = masked[k * size : (k + 1) * size]


def couple(integrals, labels, ab_pairs, cd_pairs, rows_to):
    blk = integrals.shape[0]
    tile = blk // 4
    table = labels.reshape(-1, 128)
    orbitals = jnp.concatenate([p.T.reshape(2, -1, 128) for p in (ab_pairs, cd_pairs)], axis=1)
    orbitals = orbitals.reshape(-1, 128)
    return pl.pallas_call(
        couple_kernel,
        grid_spec=pltpu.PrefetchScalarGridSpec(
            num_scalar_prefetch=1,
            grid=(4,),
            in_specs=[
                pl.BlockSpec((blk, tile), lambda i, *s: (0, i)),
                pl.BlockSpec(table.shape, lambda i, *s: (0, 0)),
                pl.BlockSpec(orbitals.shape, lambda i, *s: (0, 0)),
            ],
            out_specs=pl.BlockSpec((4, 1, tile // 4, blk), lambda i, *s: (0, i, 0, 0)),
            scratch_shapes=[pltpu.VMEM((2 * blk // 128, 128), jnp.float32)],
        ),
        out_shape=jax.ShapeDtypeStruct((4, 4, tile // 4, blk), integrals.dtype),
        compiler_params=pltpu.CompilerParams(vmem_limit_bytes=VMEM * 2**20),
        cost_estimate=pl.CostEstimate(flops=0, bytes_accessed=4 * blk * blk, transcendentals=0),
    )(rows_to, pltpu.with_memory_space_constraint(integrals, pltpu.HBM), table, orbitals)


def multiply_kernel(order_x, order_zl, coupled, *refs):
    blocks, outs, whole = refs[:4], refs[4:8], refs[8]
    depth = blocks[0].shape[0]
    size = depth // 4
    for k, ref in enumerate(blocks):
        for j in range(4):
            place = pl.multiple_of((order_x[k] * 4 + order_zl[j]) * size, 32)
            whole[pl.ds(place, size), :] = ref[j * size : (j + 1) * size, :]
    for k, out in enumerate(outs):
        rows = coupled[k * depth : (k + 1) * depth, :]
        out[...] = jnp.dot(rows, whole[...], preferred_element_type=jnp.float32).astype(out.dtype)


def multiply(coupled, blocks, order_x, order_zl):
    rows, depth = coupled.shape
    width = blocks[0].shape[1]
    part = jax.ShapeDtypeStruct((rows // 4, width), blocks[0].dtype)
    here = pl.BlockSpec(memory_space=pltpu.VMEM)
    return pl.pallas_call(
        multiply_kernel,
        in_specs=[pl.BlockSpec(memory_space=pltpu.SMEM)] * 2 + [here] * 5,
        out_specs=[here] * 4,
        scratch_shapes=[pltpu.VMEM((depth, width), blocks[0].dtype)],
        out_shape=[part] * 4,
        compiler_params=pltpu.CompilerParams(vmem_limit_bytes=VMEM * 2**20),
        cost_estimate=pl.CostEstimate(
            flops=2 * COST * rows * depth * width, bytes_accessed=rows * depth * 2, transcendentals=0
        ),
    )(as_ints(order_x), as_ints(order_zl), coupled, *blocks)


def as_ints(order):
    return jnp.stack([jnp.asarray(i, jnp.int32) for i in order])


def body(amplitudes, integrals, virt_irrep, pair_list):
    blk = integrals.shape[0]
    zh, y, x, zl, core = (lax.axis_index(a) for a in ("zh", "y", "x", "zl", "core"))

    near = gather("dir", amplitudes, "zl")
    near = jnp.concatenate(near, axis=0)

    cd_pairs = lax.dynamic_slice_in_dim(pair_list, (zh * 4 + y) * blk, blk, 0)
    ab_pairs = lax.dynamic_slice_in_dim(pair_list, (x * 4 + zl) * blk, blk, 0)
    order_zl = places("dir", zl, core)
    place_y = (jnp.arange(4, dtype=jnp.int32) - y) % 4
    coupled = couple(integrals, virt_irrep, ab_pairs, cd_pairs, place_y).reshape(blk, blk)

    if PREP_FIRST:
        near, coupled = lax.optimization_barrier((near, coupled))
    starts = [sum(WIDTHS[:k]) for k in range(len(WIDTHS))]
    product = []
    for start, width, kind in zip(starts, WIDTHS, GATHER_X):
        blocks = gather(kind, near[:, start : start + width], "x")
        product.append(multiply(coupled, blocks, places(kind, x, core), order_zl))
    done, over_ys = [], []
    earlier = None
    for part, kind in zip(product, SCATTER_Z):
        width = part[0].shape[-1]
        arrived = send(SCATTER_Y, part, "y")
        if earlier is not None and TIE:
            arrived, held = lax.optimization_barrier((arrived, earlier[1:]))
            earlier = (earlier[0], *held)
        over_y = finish(SCATTER_Y, *arrived, "y").reshape(4, -1, width)
        over_ys.append(over_y)
        if not MERGE_Z:
            blocks = pieces(over_y, places(kind, zh, core))
            if earlier is not None:
                done.append(finish(*earlier, "zh"))
            earlier = (kind, *send(kind, blocks, "zh"))
    if MERGE_Z:
        kind = SCATTER_Z[0]
        blocks = pieces(jnp.concatenate(over_ys, axis=-1), places(kind, zh, core))
        return finish(kind, *send(kind, blocks, "zh"), "zh")
    done.append(finish(*earlier, "zh"))
    return jnp.concatenate(done, axis=1)


def send(kind, blocks, axis):
    if kind == "dir":
        far = shift(blocks[2], axis, 2, -2)
        up = shift(blocks[1], axis, 1, 1)
        down = shift(blocks[3], axis, -1, -1)
        return blocks[0], far, up, down
    if kind == "rh":
        return blocks, swap(blocks[2:], axis, 1, 3)
    if kind == "rl":
        return blocks, shift(blocks[2], axis, 1, -1)
    return (lax.all_to_all(blocks, axis, 0, 0),)


def finish(kind, *arrived_axis):
    *arrived, axis = arrived_axis
    dtype = arrived[0].dtype
    if kind == "dir":
        return total(*arrived).astype(dtype)
    if kind == "rl":
        blocks, relayed = arrived
        core = lax.axis_index("core")
        add = lambda block, mine: jnp.where(mine, total(block, relayed), total(block)).astype(dtype)
        up = shift(add(blocks[1], core == 0), axis, 1, 1)
        down = shift(add(blocks[3], core == 1), axis, -1, -1)
        return total(blocks[0], up, down).astype(dtype)
    if kind == "rh":
        blocks, there = arrived
        kept = total(blocks[0], there[0])
        onward = total(blocks[1], there[1]).astype(dtype)
        return (kept + swap(onward, axis, 3, 1).astype(jnp.float32)).astype(dtype)
    return jnp.sum(arrived[0].astype(jnp.float32), axis=0).astype(dtype)


def solution(mesh):
    fine = Mesh(mesh.devices.reshape(4, 4, 4, 4, 2), ("zh", "y", "x", "zl", "core"))
    row, col = ("zh", "y"), ("x", "zl")
    placed = (P(row + col, "core"), P(row, col), P(), P())
    return jax.shard_map(
        body, mesh=fine, in_specs=placed, out_specs=P(col + row, "core"), check_vma=False
    )
```

```python
import jax
import jax.numpy as jnp
from jax import lax
from jax.experimental import pallas as pl
from jax.experimental.pallas import tpu as pltpu
from jax.sharding import Mesh, PartitionSpec as P

WIDTHS = (384, 640)
SCATTER_Z = ("rl", "rh")
VMEM = 32


def permute(block, axis, target):
    moves = [(i * 2 + core, target(i, core) % 4 * 2 + core) for i in range(4) for core in (0, 1)]
    return lax.ppermute(block, (axis, "core"), moves)


def shift(block, axis, first, second):
    return permute(block, axis, lambda i, core: i + (second if core else first))


def swap(block, axis, first, second):
    return permute(block, axis, lambda i, core: i ^ (second if core else first))


def total(*terms):
    return sum(t.astype(jnp.float32) for t in terms)


def places(kind, me, core):
    if kind in ("dir", "rl"):
        return [(me + d) % 4 for d in range(4)]
    near = jnp.where(core == 0, 3, 1)
    return [me, me ^ near, me ^ near ^ 2, me ^ 2]


def gather(own, axis):
    far = shift(own, axis, 2, -2)
    after = shift(own, axis, -1, -1)
    return [own, after, far, shift(own, axis, 1, 1)]


def pieces(blocks, order):
    return jnp.stack([lax.dynamic_index_in_dim(blocks, i, 0, keepdims=False) for i in order])


def lookup(table, index):
    found = jnp.zeros(index.shape, table.dtype)
    for row in range(table.shape[0]):
        line = jnp.broadcast_to(table[row : row + 1, :], index.shape)
        value = jnp.take_along_axis(line, index & 127, axis=1)
        found = jnp.where(index >> 7 == row, value, found)
    return found


def couple_kernel(rows_to, block, table, orbitals, out, done, labels):
    step = pl.program_id(0)
    tile, blk = block.shape[1], block.shape[0]
    lines = blk // 128

    @pl.when(step == 0)
    def _():
        symmetry = lookup(table[...], orbitals[...]).astype(jnp.float32)
        first, second = symmetry[: 2 * lines].astype(jnp.int32), symmetry[2 * lines :].astype(jnp.int32)
        labels[...] = jnp.bitwise_xor(first, second).astype(jnp.float32)

    done[...] = jnp.zeros(done.shape, done.dtype)
    mine = []
    for k in range(tile // 128):
        line = labels[pl.ds(step * (tile // 128) + k, 1), :]
        mine.append(jnp.broadcast_to(line, (128, 128)).T.astype(block.dtype))
    mine = jnp.concatenate(mine, axis=0)
    turned = block[...].T
    size = tile // 4
    for j in range(lines):
        across = slice(j * 128, (j + 1) * 128)
        other = labels[lines + j : lines + j + 1, :].astype(block.dtype)
        masked = jnp.where(mine == other, turned[:, across], jnp.zeros((), block.dtype))
        for k in range(4):
            out[rows_to[k], 0, :, across] = masked[k * size : (k + 1) * size]


def couple(integrals, labels, ab_pairs, cd_pairs, rows_to):
    blk = integrals.shape[0]
    tile = blk // 4
    table = labels.reshape(-1, 128)
    orbitals = jnp.concatenate([p.T.reshape(2, -1, 128) for p in (ab_pairs, cd_pairs)], axis=1)
    orbitals = orbitals.reshape(-1, 128)
    return pl.pallas_call(
        couple_kernel,
        grid_spec=pltpu.PrefetchScalarGridSpec(
            num_scalar_prefetch=1,
            grid=(4,),
            in_specs=[
                pl.BlockSpec((blk, tile), lambda i, *s: (0, i)),
                pl.BlockSpec(table.shape, lambda i, *s: (0, 0)),
                pl.BlockSpec(orbitals.shape, lambda i, *s: (0, 0)),
            ],
            out_specs=[
                pl.BlockSpec((4, 1, tile // 4, blk), lambda i, *s: (0, i, 0, 0)),
                pl.BlockSpec((8, 128), lambda i, *s: (0, 0)),
            ],
            scratch_shapes=[pltpu.VMEM((2 * blk // 128, 128), jnp.float32)],
        ),
        out_shape=[
            jax.ShapeDtypeStruct((4, 4, tile // 4, blk), integrals.dtype),
            jax.ShapeDtypeStruct((8, 128), jnp.float32),
        ],
        compiler_params=pltpu.CompilerParams(vmem_limit_bytes=VMEM * 2**20),
        cost_estimate=pl.CostEstimate(flops=0, bytes_accessed=4 * blk * blk, transcendentals=0),
    )(rows_to, pltpu.with_memory_space_constraint(integrals, pltpu.HBM), table, orbitals)


def multiply_kernel(order, coupled, *refs):
    *blocks, out, whole = refs
    depth = blocks[0].shape[0]

    @pl.when(pl.program_id(0) == 0)
    def _():
        for k, ref in enumerate(blocks):
            whole[pl.ds(pl.multiple_of(order[k] * depth, 128), depth), :] = ref[...]

    out[...] = jnp.dot(coupled[...], whole[...], preferred_element_type=jnp.float32).astype(out.dtype)[None]


def multiply(coupled, blocks, order):
    rows, depth = coupled.shape
    width = blocks[0].shape[1]
    tile = rows // 4
    one = pl.BlockSpec(blocks[0].shape, lambda i, s: (0, 0))
    return pl.pallas_call(
        multiply_kernel,
        grid_spec=pltpu.PrefetchScalarGridSpec(
            num_scalar_prefetch=1,
            grid=(4,),
            in_specs=[pl.BlockSpec((tile, depth), lambda i, s: (i, 0))] + [one] * 4,
            out_specs=pl.BlockSpec((1, tile, width), lambda i, s: (i, 0, 0)),
            scratch_shapes=[pltpu.VMEM((depth, width), blocks[0].dtype)],
        ),
        out_shape=jax.ShapeDtypeStruct((4, tile, width), blocks[0].dtype),
        compiler_params=pltpu.CompilerParams(vmem_limit_bytes=VMEM * 2**20),
        cost_estimate=pl.CostEstimate(
            flops=2 * rows * depth * width, bytes_accessed=rows * depth * 2, transcendentals=0
        ),
    )(as_ints(order), coupled, *blocks)


def as_ints(order):
    return jnp.stack([jnp.asarray(i).astype(jnp.int32) for i in order])


def body(amplitudes, integrals, virt_irrep, pair_list):
    blk = integrals.shape[0]
    zh, y, x, zl, core = (lax.axis_index(a) for a in ("zh", "y", "x", "zl", "core"))

    near = lax.all_gather(amplitudes, "zl", axis=0, tiled=True)

    cd_pairs = lax.dynamic_slice_in_dim(pair_list, (zh * 4 + y) * blk, blk, 0)
    ab_pairs = lax.dynamic_slice_in_dim(pair_list, (x * 4 + zl) * blk, blk, 0)
    order_y = places("dir", y, core)
    place_y = as_ints([sum(k * (order_y[k] == to) for k in range(4)) for to in range(4)])
    coupled, masked = couple(integrals, virt_irrep, ab_pairs, cd_pairs, place_y)
    coupled = coupled.reshape(blk, blk)

    product, start = [], 0
    for width in WIDTHS:
        part = near[:, start : start + width]
        if start:
            part, masked = lax.optimization_barrier((part, masked))
        start += width
        product.append(multiply(coupled, gather(part, "x"), places("dir", x, core)))

    done, earlier = [], None
    for part, kind in zip(product, SCATTER_Z):
        arrived = send("dir", part, "y")
        if earlier is not None:
            arrived, held = lax.optimization_barrier((arrived, earlier[1:]))
            earlier = (earlier[0], *held)
        over_y = finish("dir", *arrived, "y").reshape(4, -1, part.shape[-1])
        blocks = pieces(over_y, places(kind, zh, core))
        if earlier is not None:
            done.append(finish(*earlier, "zh"))
        earlier = (kind, *send(kind, blocks, "zh"))
    done.append(finish(*earlier, "zh"))
    return jnp.concatenate(done, axis=1)


def send(kind, blocks, axis):
    if kind == "dir":
        far = shift(blocks[2], axis, 2, -2)
        up = shift(blocks[1], axis, 1, 1)
        down = shift(blocks[3], axis, -1, -1)
        return blocks[0], far, up, down
    if kind == "rh":
        return blocks, swap(blocks[2:], axis, 1, 3)
    return blocks, shift(blocks[2], axis, 1, -1)


def finish(kind, *arrived_axis):
    *arrived, axis = arrived_axis
    dtype = arrived[0].dtype
    if kind == "dir":
        return total(*arrived).astype(dtype)
    if kind == "rl":
        blocks, relayed = arrived
        core = lax.axis_index("core")
        add = lambda block, mine: jnp.where(mine, total(block, relayed), total(block)).astype(dtype)
        up = shift(add(blocks[1], core == 0), axis, 1, 1)
        down = shift(add(blocks[3], core == 1), axis, -1, -1)
        return total(blocks[0], up, down).astype(dtype)
    blocks, there = arrived
    kept = total(blocks[0], there[0])
    onward = total(blocks[1], there[1]).astype(dtype)
    return (kept + swap(onward, axis, 3, 1).astype(jnp.float32)).astype(dtype)


def solution(mesh):
    fine = Mesh(mesh.devices.reshape(4, 4, 4, 4, 2), ("zh", "y", "x", "zl", "core"))
    row, col = ("zh", "y"), ("x", "zl")
    placed = (P(row + col, "core"), P(row, col), P(), P())
    return jax.shard_map(
        body, mesh=fine, in_specs=placed, out_specs=P(col + row, "core"), check_vma=False
    )
```

```python
import jax
import jax.numpy as jnp
from jax import lax
from jax.experimental import pallas as pl
from jax.experimental.pallas import tpu as pltpu
from jax.sharding import Mesh, PartitionSpec as P

WIDTHS = (384, 640)
SCATTER_Z = ("rh", "rh")
VMEM = 32


def permute(block, axis, target):
    moves = [(i * 2 + core, target(i, core) % 4 * 2 + core) for i in range(4) for core in (0, 1)]
    return lax.ppermute(block, (axis, "core"), moves)


def shift(block, axis, first, second):
    return permute(block, axis, lambda i, core: i + (second if core else first))


def swap(block, axis, first, second):
    return permute(block, axis, lambda i, core: i ^ (second if core else first))


def total(*terms):
    return sum(t.astype(jnp.float32) for t in terms)


def places(kind, me, core):
    if kind in ("dir", "rl"):
        return [(me + d) % 4 for d in range(4)]
    near = jnp.where(core == 0, 3, 1)
    return [me, me ^ near, me ^ near ^ 2, me ^ 2]


def gather(own, axis):
    far = shift(own, axis, 2, -2)
    after = shift(own, axis, -1, -1)
    return [own, after, far, shift(own, axis, 1, 1)]


def pieces(blocks, order):
    return jnp.stack([lax.dynamic_index_in_dim(blocks, i, 0, keepdims=False) for i in order])


def lookup(table, index):
    found = jnp.zeros(index.shape, table.dtype)
    for row in range(table.shape[0]):
        line = jnp.broadcast_to(table[row : row + 1, :], index.shape)
        value = jnp.take_along_axis(line, index & 127, axis=1)
        found = jnp.where(index >> 7 == row, value, found)
    return found


def couple_kernel(rows_to, block, table, orbitals, out, done, labels):
    step = pl.program_id(0)
    tile, blk = block.shape[1], block.shape[0]
    lines = blk // 128

    @pl.when(step == 0)
    def _():
        symmetry = lookup(table[...], orbitals[...]).astype(jnp.float32)
        first, second = symmetry[: 2 * lines].astype(jnp.int32), symmetry[2 * lines :].astype(jnp.int32)
        labels[...] = jnp.bitwise_xor(first, second).astype(jnp.float32)

    done[...] = jnp.zeros(done.shape, done.dtype)
    mine = []
    for k in range(tile // 128):
        line = labels[pl.ds(step * (tile // 128) + k, 1), :]
        mine.append(jnp.broadcast_to(line, (128, 128)).T.astype(block.dtype))
    mine = jnp.concatenate(mine, axis=0)
    turned = block[...].T
    size = tile // 4
    for j in range(lines):
        across = slice(j * 128, (j + 1) * 128)
        other = labels[lines + j : lines + j + 1, :].astype(block.dtype)
        masked = jnp.where(mine == other, turned[:, across], jnp.zeros((), block.dtype))
        for k in range(4):
            out[rows_to[k], 0, :, across] = masked[k * size : (k + 1) * size]


def couple(integrals, labels, ab_pairs, cd_pairs, rows_to):
    blk = integrals.shape[0]
    tile = blk // 4
    table = labels.reshape(-1, 128)
    orbitals = jnp.concatenate([p.T.reshape(2, -1, 128) for p in (ab_pairs, cd_pairs)], axis=1)
    orbitals = orbitals.reshape(-1, 128)
    return pl.pallas_call(
        couple_kernel,
        grid_spec=pltpu.PrefetchScalarGridSpec(
            num_scalar_prefetch=1,
            grid=(4,),
            in_specs=[
                pl.BlockSpec((blk, tile), lambda i, *s: (0, i)),
                pl.BlockSpec(table.shape, lambda i, *s: (0, 0)),
                pl.BlockSpec(orbitals.shape, lambda i, *s: (0, 0)),
            ],
            out_specs=[
                pl.BlockSpec((4, 1, tile // 4, blk), lambda i, *s: (0, i, 0, 0)),
                pl.BlockSpec((8, 128), lambda i, *s: (0, 0)),
            ],
            scratch_shapes=[pltpu.VMEM((2 * blk // 128, 128), jnp.float32)],
        ),
        out_shape=[
            jax.ShapeDtypeStruct((4, 4, tile // 4, blk), integrals.dtype),
            jax.ShapeDtypeStruct((8, 128), jnp.float32),
        ],
        compiler_params=pltpu.CompilerParams(vmem_limit_bytes=VMEM * 2**20),
        cost_estimate=pl.CostEstimate(flops=0, bytes_accessed=4 * blk * blk, transcendentals=0),
    )(rows_to, pltpu.with_memory_space_constraint(integrals, pltpu.HBM), table, orbitals)


def multiply_kernel(order, coupled, *refs):
    *blocks, out, whole = refs
    depth = blocks[0].shape[0]

    @pl.when(pl.program_id(0) == 0)
    def _():
        for k, ref in enumerate(blocks):
            whole[pl.ds(pl.multiple_of(order[k] * depth, 128), depth), :] = ref[...]

    out[...] = jnp.dot(coupled[...], whole[...], preferred_element_type=jnp.float32).astype(out.dtype)[None]


def multiply(coupled, blocks, order):
    rows, depth = coupled.shape
    width = blocks[0].shape[1]
    tile = rows // 4
    one = pl.BlockSpec(blocks[0].shape, lambda i, s: (0, 0))
    return pl.pallas_call(
        multiply_kernel,
        grid_spec=pltpu.PrefetchScalarGridSpec(
            num_scalar_prefetch=1,
            grid=(4,),
            in_specs=[pl.BlockSpec((tile, depth), lambda i, s: (i, 0))] + [one] * 4,
            out_specs=pl.BlockSpec((1, tile, width), lambda i, s: (i, 0, 0)),
            scratch_shapes=[pltpu.VMEM((depth, width), blocks[0].dtype)],
        ),
        out_shape=jax.ShapeDtypeStruct((4, tile, width), blocks[0].dtype),
        compiler_params=pltpu.CompilerParams(vmem_limit_bytes=VMEM * 2**20),
        cost_estimate=pl.CostEstimate(
            flops=2 * rows * depth * width, bytes_accessed=rows * depth * 2, transcendentals=0
        ),
    )(as_ints(order), coupled, *blocks)


def as_ints(order):
    return jnp.stack([jnp.asarray(i).astype(jnp.int32) for i in order])


def body(amplitudes, integrals, virt_irrep, pair_list):
    blk = integrals.shape[0]
    zh, y, x, zl, core = (lax.axis_index(a) for a in ("zh", "y", "x", "zl", "core"))

    near = lax.all_gather(amplitudes, "zl", axis=0, tiled=True)

    cd_pairs = lax.dynamic_slice_in_dim(pair_list, (zh * 4 + y) * blk, blk, 0)
    ab_pairs = lax.dynamic_slice_in_dim(pair_list, (x * 4 + zl) * blk, blk, 0)
    order_y = places("dir", y, core)
    place_y = as_ints([sum(k * (order_y[k] == to) for k in range(4)) for to in range(4)])
    coupled, masked = couple(integrals, virt_irrep, ab_pairs, cd_pairs, place_y)
    coupled = coupled.reshape(blk, blk)

    product, start = [], 0
    for width in WIDTHS:
        part = near[:, start : start + width]
        if start:
            part, masked = lax.optimization_barrier((part, masked))
        start += width
        product.append(multiply(coupled, gather(part, "x"), places("dir", x, core)))

    done, earlier = [], None
    for part, kind in zip(product, SCATTER_Z):
        arrived = send("dir", part, "y")
        if earlier is not None:
            arrived, held = lax.optimization_barrier((arrived, earlier[1:]))
            earlier = (earlier[0], *held)
        over_y = finish("dir", *arrived, "y").reshape(4, -1, part.shape[-1])
        blocks = pieces(over_y, places(kind, zh, core))
        if earlier is not None:
            done.append(finish(*earlier, "zh"))
        earlier = (kind, *send(kind, blocks, "zh"))
    done.append(finish(*earlier, "zh"))
    return jnp.concatenate(done, axis=1)


def send(kind, blocks, axis):
    if kind == "dir":
        far = shift(blocks[2], axis, 2, -2)
        up = shift(blocks[1], axis, 1, 1)
        down = shift(blocks[3], axis, -1, -1)
        return blocks[0], far, up, down
    if kind == "rh":
        return blocks, swap(blocks[2:], axis, 1, 3)
    return blocks, shift(blocks[2], axis, 1, -1)


def finish(kind, *arrived_axis):
    *arrived, axis = arrived_axis
    dtype = arrived[0].dtype
    if kind == "dir":
        return total(*arrived).astype(dtype)
    if kind == "rl":
        blocks, relayed = arrived
        core = lax.axis_index("core")
        add = lambda block, mine: jnp.where(mine, total(block, relayed), total(block)).astype(dtype)
        up = shift(add(blocks[1], core == 0), axis, 1, 1)
        down = shift(add(blocks[3], core == 1), axis, -1, -1)
        return total(blocks[0], up, down).astype(dtype)
    blocks, there = arrived
    kept = total(blocks[0], there[0])
    onward = total(blocks[1], there[1]).astype(dtype)
    return (kept + swap(onward, axis, 3, 1).astype(jnp.float32)).astype(dtype)


def solution(mesh):
    fine = Mesh(mesh.devices.reshape(4, 4, 4, 4, 2), ("zh", "y", "x", "zl", "core"))
    row, col = ("zh", "y"), ("x", "zl")
    placed = (P(row + col, "core"), P(row, col), P(), P())
    return jax.shard_map(
        body, mesh=fine, in_specs=placed, out_specs=P(col + row, "core"), check_vma=False
    )
```

```python
import jax
import jax.numpy as jnp
from jax import lax
from jax.experimental import pallas as pl
from jax.experimental.pallas import tpu as pltpu
from jax.sharding import Mesh, PartitionSpec as P

WIDTHS = (384, 640)
SCATTER_Z = ("rh", "rh")
VMEM = 32


def permute(block, axis, target):
    moves = [(i * 2 + core, target(i, core) % 4 * 2 + core) for i in range(4) for core in (0, 1)]
    return lax.ppermute(block, (axis, "core"), moves)


def shift(block, axis, first, second):
    return permute(block, axis, lambda i, core: i + (second if core else first))


def swap(block, axis, first, second):
    return permute(block, axis, lambda i, core: i ^ (second if core else first))


def total(*terms):
    return sum(t.astype(jnp.float32) for t in terms)


def places(kind, me, core):
    if kind in ("dir", "rl"):
        return [(me + d) % 4 for d in range(4)]
    near = jnp.where(core == 0, 3, 1)
    return [me, me ^ near, me ^ near ^ 2, me ^ 2]


def gather(own, axis):
    far = shift(own, axis, 2, -2)
    after = shift(own, axis, -1, -1)
    return [own, after, far, shift(own, axis, 1, 1)]


def pieces(blocks, order):
    return jnp.stack([lax.dynamic_index_in_dim(blocks, i, 0, keepdims=False) for i in order])


def lookup(table, index):
    found = jnp.zeros(index.shape, table.dtype)
    for row in range(table.shape[0]):
        line = jnp.broadcast_to(table[row : row + 1, :], index.shape)
        value = jnp.take_along_axis(line, index & 127, axis=1)
        found = jnp.where(index >> 7 == row, value, found)
    return found


def couple_kernel(rows_to, block, table, orbitals, out, done, labels):
    step = pl.program_id(0)
    tile, blk = block.shape[1], block.shape[0]
    lines = blk // 128

    @pl.when(step == 0)
    def _():
        symmetry = lookup(table[...], orbitals[...]).astype(jnp.float32)
        first, second = symmetry[: 2 * lines].astype(jnp.int32), symmetry[2 * lines :].astype(jnp.int32)
        labels[...] = jnp.bitwise_xor(first, second).astype(jnp.float32)

    done[...] = jnp.zeros(done.shape, done.dtype)
    mine = []
    for k in range(tile // 128):
        line = labels[pl.ds(step * (tile // 128) + k, 1), :]
        mine.append(jnp.broadcast_to(line, (128, 128)).T.astype(block.dtype))
    mine = jnp.concatenate(mine, axis=0)
    turned = block[...].T
    size = tile // 4
    for j in range(lines):
        across = slice(j * 128, (j + 1) * 128)
        other = labels[lines + j : lines + j + 1, :].astype(block.dtype)
        masked = jnp.where(mine == other, turned[:, across], jnp.zeros((), block.dtype))
        for k in range(4):
            out[rows_to[k], 0, :, across] = masked[k * size : (k + 1) * size]


def couple(integrals, labels, ab_pairs, cd_pairs, rows_to):
    blk = integrals.shape[0]
    tile = blk // 4
    table = labels.reshape(-1, 128)
    orbitals = jnp.concatenate([p.T.reshape(2, -1, 128) for p in (ab_pairs, cd_pairs)], axis=1)
    orbitals = orbitals.reshape(-1, 128)
    return pl.pallas_call(
        couple_kernel,
        grid_spec=pltpu.PrefetchScalarGridSpec(
            num_scalar_prefetch=1,
            grid=(4,),
            in_specs=[
                pl.BlockSpec((blk, tile), lambda i, *s: (0, i)),
                pl.BlockSpec(table.shape, lambda i, *s: (0, 0)),
                pl.BlockSpec(orbitals.shape, lambda i, *s: (0, 0)),
            ],
            out_specs=[
                pl.BlockSpec((4, 1, tile // 4, blk), lambda i, *s: (0, i, 0, 0)),
                pl.BlockSpec((8, 128), lambda i, *s: (0, 0)),
            ],
            scratch_shapes=[pltpu.VMEM((2 * blk // 128, 128), jnp.float32)],
        ),
        out_shape=[
            jax.ShapeDtypeStruct((4, 4, tile // 4, blk), integrals.dtype),
            jax.ShapeDtypeStruct((8, 128), jnp.float32),
        ],
        compiler_params=pltpu.CompilerParams(vmem_limit_bytes=VMEM * 2**20),
        cost_estimate=pl.CostEstimate(flops=0, bytes_accessed=4 * blk * blk, transcendentals=0),
    )(rows_to, pltpu.with_memory_space_constraint(integrals, pltpu.HBM), table, orbitals)


def multiply_kernel(order, coupled, *refs):
    *blocks, out, whole = refs
    depth = blocks[0].shape[0]

    @pl.when(pl.program_id(0) == 0)
    def _():
        for k, ref in enumerate(blocks):
            whole[pl.ds(pl.multiple_of(order[k] * depth, 128), depth), :] = ref[...]

    out[...] = jnp.dot(coupled[...], whole[...], preferred_element_type=jnp.float32).astype(out.dtype)[None]


def multiply(coupled, blocks, order, first):
    rows, depth = coupled.shape
    width = blocks[0].shape[1]
    tile = rows // 4
    one = pl.BlockSpec(blocks[0].shape, lambda i, s: (0, 0))
    return pl.pallas_call(
        multiply_kernel,
        grid_spec=pltpu.PrefetchScalarGridSpec(
            num_scalar_prefetch=1,
            grid=(2,),
            in_specs=[pl.BlockSpec((tile, depth), lambda i, s: ((i + first) % 4, 0))] + [one] * 4,
            out_specs=pl.BlockSpec((1, tile, width), lambda i, s: (i, 0, 0)),
            scratch_shapes=[pltpu.VMEM((depth, width), blocks[0].dtype)],
        ),
        out_shape=jax.ShapeDtypeStruct((2, tile, width), blocks[0].dtype),
        compiler_params=pltpu.CompilerParams(vmem_limit_bytes=VMEM * 2**20),
        cost_estimate=pl.CostEstimate(
            flops=rows * depth * width, bytes_accessed=rows * depth, transcendentals=0
        ),
    )(as_ints(order), coupled, *blocks)


def as_ints(order):
    return jnp.stack([jnp.asarray(i).astype(jnp.int32) for i in order])


def body(amplitudes, integrals, virt_irrep, pair_list):
    blk = integrals.shape[0]
    zh, y, x, zl, core = (lax.axis_index(a) for a in ("zh", "y", "x", "zl", "core"))

    near = lax.all_gather(amplitudes, "zl", axis=0, tiled=True)

    cd_pairs = lax.dynamic_slice_in_dim(pair_list, (zh * 4 + y) * blk, blk, 0)
    ab_pairs = lax.dynamic_slice_in_dim(pair_list, (x * 4 + zl) * blk, blk, 0)
    order_y = places("dir", y, core)
    place_y = as_ints([sum(k * (order_y[k] == to) for k in range(4)) for to in range(4)])
    coupled, masked = couple(integrals, virt_irrep, ab_pairs, cd_pairs, place_y)
    coupled = coupled.reshape(blk, blk)

    product, start = [], 0
    for width in WIDTHS:
        part = near[:, start : start + width]
        if start:
            part, masked = lax.optimization_barrier((part, masked))
        start += width
        blocks, order = gather(part, "x"), places("dir", x, core)
        up, far = multiply(coupled, blocks, order, 1)
        down, own = multiply(coupled, blocks, order, 3)
        product.append((own, up, far, down))

    done, earlier = [], None
    for part, kind in zip(product, SCATTER_Z):
        arrived = send("dir", part, "y")
        if earlier is not None:
            arrived, held = lax.optimization_barrier((arrived, earlier[1:]))
            earlier = (earlier[0], *held)
        over_y = finish("dir", *arrived, "y").reshape(4, -1, part[0].shape[-1])
        blocks = pieces(over_y, places(kind, zh, core))
        if earlier is not None:
            done.append(finish(*earlier, "zh"))
        earlier = (kind, *send(kind, blocks, "zh"))
    done.append(finish(*earlier, "zh"))
    return jnp.concatenate(done, axis=1)


def send(kind, blocks, axis):
    if kind == "dir":
        far = shift(blocks[2], axis, 2, -2)
        up = shift(blocks[1], axis, 1, 1)
        down = shift(blocks[3], axis, -1, -1)
        return blocks[0], far, up, down
    if kind == "rh":
        return blocks, swap(blocks[2:], axis, 1, 3)
    return blocks, shift(blocks[2], axis, 1, -1)


def finish(kind, *arrived_axis):
    *arrived, axis = arrived_axis
    dtype = arrived[0].dtype
    if kind == "dir":
        return total(*arrived).astype(dtype)
    if kind == "rl":
        blocks, relayed = arrived
        core = lax.axis_index("core")
        add = lambda block, mine: jnp.where(mine, total(block, relayed), total(block)).astype(dtype)
        up = shift(add(blocks[1], core == 0), axis, 1, 1)
        down = shift(add(blocks[3], core == 1), axis, -1, -1)
        return total(blocks[0], up, down).astype(dtype)
    blocks, there = arrived
    kept = total(blocks[0], there[0])
    onward = total(blocks[1], there[1]).astype(dtype)
    return (kept + swap(onward, axis, 3, 1).astype(jnp.float32)).astype(dtype)


def solution(mesh):
    fine = Mesh(mesh.devices.reshape(4, 4, 4, 4, 2), ("zh", "y", "x", "zl", "core"))
    row, col = ("zh", "y"), ("x", "zl")
    placed = (P(row + col, "core"), P(row, col), P(), P())
    return jax.shard_map(
        body, mesh=fine, in_specs=placed, out_specs=P(col + row, "core"), check_vma=False
    )
```

```python
import jax
import jax.numpy as jnp
from jax import lax
from jax.experimental import pallas as pl
from jax.experimental.pallas import tpu as pltpu
from jax.sharding import Mesh, PartitionSpec as P

WIDTHS = (384, 640)
SCATTER_Z = ("rh", "rh")
VMEM = 32


def permute(block, axis, target):
    moves = [(i * 2 + core, target(i, core) % 4 * 2 + core) for i in range(4) for core in (0, 1)]
    return lax.ppermute(block, (axis, "core"), moves)


def shift(block, axis, first, second):
    return permute(block, axis, lambda i, core: i + (second if core else first))


def swap(block, axis, first, second):
    return permute(block, axis, lambda i, core: i ^ (second if core else first))


def total(*terms):
    return sum(t.astype(jnp.float32) for t in terms)


def places(kind, me, core):
    if kind in ("dir", "rl"):
        return [(me + d) % 4 for d in range(4)]
    near = jnp.where(core == 0, 3, 1)
    return [me, me ^ near, me ^ near ^ 2, me ^ 2]


def gather(own, axis):
    far = shift(own, axis, 2, -2)
    after = shift(own, axis, -1, -1)
    return [own, after, far, shift(own, axis, 1, 1)]


def pieces(blocks, order):
    return jnp.stack([lax.dynamic_index_in_dim(blocks, i, 0, keepdims=False) for i in order])


def lookup(table, index):
    found = jnp.zeros(index.shape, table.dtype)
    for row in range(table.shape[0]):
        line = jnp.broadcast_to(table[row : row + 1, :], index.shape)
        value = jnp.take_along_axis(line, index & 127, axis=1)
        found = jnp.where(index >> 7 == row, value, found)
    return found


def couple_kernel(rows_to, block, table, orbitals, out, done, labels):
    step = pl.program_id(0)
    tile, blk = block.shape[1], block.shape[0]
    lines = blk // 128

    @pl.when(step == 0)
    def _():
        symmetry = lookup(table[...], orbitals[...]).astype(jnp.float32)
        first, second = symmetry[: 2 * lines].astype(jnp.int32), symmetry[2 * lines :].astype(jnp.int32)
        labels[...] = jnp.bitwise_xor(first, second).astype(jnp.float32)

    done[...] = jnp.zeros(done.shape, done.dtype)
    mine = []
    for k in range(tile // 128):
        line = labels[pl.ds(step * (tile // 128) + k, 1), :]
        mine.append(jnp.broadcast_to(line, (128, 128)).T.astype(block.dtype))
    mine = jnp.concatenate(mine, axis=0)
    turned = block[...].T
    size = tile // 4
    for j in range(lines):
        across = slice(j * 128, (j + 1) * 128)
        other = labels[lines + j : lines + j + 1, :].astype(block.dtype)
        masked = jnp.where(mine == other, turned[:, across], jnp.zeros((), block.dtype))
        for k in range(4):
            out[rows_to[k], 0, :, across] = masked[k * size : (k + 1) * size]


def couple(integrals, labels, ab_pairs, cd_pairs, rows_to):
    blk = integrals.shape[0]
    tile = blk // 4
    table = labels.reshape(-1, 128)
    orbitals = jnp.concatenate([p.T.reshape(2, -1, 128) for p in (ab_pairs, cd_pairs)], axis=1)
    orbitals = orbitals.reshape(-1, 128)
    return pl.pallas_call(
        couple_kernel,
        grid_spec=pltpu.PrefetchScalarGridSpec(
            num_scalar_prefetch=1,
            grid=(4,),
            in_specs=[
                pl.BlockSpec((blk, tile), lambda i, *s: (0, i)),
                pl.BlockSpec(table.shape, lambda i, *s: (0, 0)),
                pl.BlockSpec(orbitals.shape, lambda i, *s: (0, 0)),
            ],
            out_specs=[
                pl.BlockSpec((4, 1, tile // 4, blk), lambda i, *s: (0, i, 0, 0)),
                pl.BlockSpec((8, 128), lambda i, *s: (0, 0)),
            ],
            scratch_shapes=[pltpu.VMEM((2 * blk // 128, 128), jnp.float32)],
        ),
        out_shape=[
            jax.ShapeDtypeStruct((4, 4, tile // 4, blk), integrals.dtype),
            jax.ShapeDtypeStruct((8, 128), jnp.float32),
        ],
        compiler_params=pltpu.CompilerParams(vmem_limit_bytes=VMEM * 2**20),
        cost_estimate=pl.CostEstimate(flops=0, bytes_accessed=4 * blk * blk, transcendentals=0),
    )(rows_to, pltpu.with_memory_space_constraint(integrals, pltpu.HBM), table, orbitals)


def multiply_kernel(order, coupled, *refs):
    *blocks, out, whole = refs
    depth = blocks[0].shape[0]

    @pl.when(pl.program_id(0) == 0)
    def _():
        for k, ref in enumerate(blocks):
            whole[pl.ds(pl.multiple_of(order[k] * depth, 128), depth), :] = ref[...]

    out[...] = jnp.dot(coupled[...], whole[...], preferred_element_type=jnp.float32).astype(out.dtype)[None]


def multiply(coupled, blocks, order, first, count):
    rows, depth = coupled.shape
    width = blocks[0].shape[1]
    tile = rows // 4
    one = pl.BlockSpec(blocks[0].shape, lambda i, s: (0, 0))
    return pl.pallas_call(
        multiply_kernel,
        grid_spec=pltpu.PrefetchScalarGridSpec(
            num_scalar_prefetch=1,
            grid=(count,),
            in_specs=[pl.BlockSpec((tile, depth), lambda i, s: ((i + first) % 4, 0))] + [one] * 4,
            out_specs=pl.BlockSpec((1, tile, width), lambda i, s: (i, 0, 0)),
            scratch_shapes=[pltpu.VMEM((depth, width), blocks[0].dtype)],
        ),
        out_shape=jax.ShapeDtypeStruct((count, tile, width), blocks[0].dtype),
        compiler_params=pltpu.CompilerParams(vmem_limit_bytes=VMEM * 2**20),
        cost_estimate=pl.CostEstimate(
            flops=count * tile * depth * width * 2, bytes_accessed=count * tile * depth * 2, transcendentals=0
        ),
    )(as_ints(order), coupled, *blocks)


def as_ints(order):
    return jnp.stack([jnp.asarray(i).astype(jnp.int32) for i in order])


def body(amplitudes, integrals, virt_irrep, pair_list):
    blk = integrals.shape[0]
    zh, y, x, zl, core = (lax.axis_index(a) for a in ("zh", "y", "x", "zl", "core"))

    near = lax.all_gather(amplitudes, "zl", axis=0, tiled=True)

    cd_pairs = lax.dynamic_slice_in_dim(pair_list, (zh * 4 + y) * blk, blk, 0)
    ab_pairs = lax.dynamic_slice_in_dim(pair_list, (x * 4 + zl) * blk, blk, 0)
    order_y = places("dir", y, core)
    place_y = as_ints([sum(k * (order_y[k] == to) for k in range(4)) for to in range(4)])
    coupled, masked = couple(integrals, virt_irrep, ab_pairs, cd_pairs, place_y)
    coupled = coupled.reshape(blk, blk)

    product, start = [], 0
    for width in WIDTHS:
        part = near[:, start : start + width]
        if start:
            part, masked = lax.optimization_barrier((part, masked))
        start += width
        blocks, order = gather(part, "x"), places("dir", x, core)
        if product:
            product.append(tuple(multiply(coupled, blocks, order, 0, 4)))
        else:
            up, far = multiply(coupled, blocks, order, 1, 2)
            down, own = multiply(coupled, blocks, order, 3, 2)
            product.append((own, up, far, down))

    done, earlier = [], None
    for part, kind in zip(product, SCATTER_Z):
        arrived = send("dir", part, "y")
        if earlier is not None:
            arrived, held = lax.optimization_barrier((arrived, earlier[1:]))
            earlier = (earlier[0], *held)
        over_y = finish("dir", *arrived, "y").reshape(4, -1, part[0].shape[-1])
        blocks = pieces(over_y, places(kind, zh, core))
        if earlier is not None:
            done.append(finish(*earlier, "zh"))
        earlier = (kind, *send(kind, blocks, "zh"))
    done.append(finish(*earlier, "zh"))
    return jnp.concatenate(done, axis=1)


def send(kind, blocks, axis):
    if kind == "dir":
        far = shift(blocks[2], axis, 2, -2)
        up = shift(blocks[1], axis, 1, 1)
        down = shift(blocks[3], axis, -1, -1)
        return blocks[0], far, up, down
    if kind == "rh":
        return blocks, swap(blocks[2:], axis, 1, 3)
    return blocks, shift(blocks[2], axis, 1, -1)


def finish(kind, *arrived_axis):
    *arrived, axis = arrived_axis
    dtype = arrived[0].dtype
    if kind == "dir":
        return total(*arrived).astype(dtype)
    if kind == "rl":
        blocks, relayed = arrived
        core = lax.axis_index("core")
        add = lambda block, mine: jnp.where(mine, total(block, relayed), total(block)).astype(dtype)
        up = shift(add(blocks[1], core == 0), axis, 1, 1)
        down = shift(add(blocks[3], core == 1), axis, -1, -1)
        return total(blocks[0], up, down).astype(dtype)
    blocks, there = arrived
    kept = total(blocks[0], there[0])
    onward = total(blocks[1], there[1]).astype(dtype)
    return (kept + swap(onward, axis, 3, 1).astype(jnp.float32)).astype(dtype)


def solution(mesh):
    fine = Mesh(mesh.devices.reshape(4, 4, 4, 4, 2), ("zh", "y", "x", "zl", "core"))
    row, col = ("zh", "y"), ("x", "zl")
    placed = (P(row + col, "core"), P(row, col), P(), P())
    return jax.shard_map(
        body, mesh=fine, in_specs=placed, out_specs=P(col + row, "core"), check_vma=False
    )
```
